32 devices in a mesh: groups: 2 (over x), node: 16 (over z, y, core).
Axes of the slice: x: 2, y: 2, z: 4, core: 2. Of those that a mesh axis runs over, the one named last changes fastest.
Arguments:
- tokens: bfloat16 [2048, 4096], P(('groups', 'node')), parts along dimension 0, may hold values from -6 to 6
- routes: int32 [2048, 8], P(('groups', 'node')), parts along dimension 0, may hold values from 0 to 15, all different within a row; in each aligned block of 64 rows (0 to 63, 64 to 127, ...) at most 48 rows name the same one
- gate_codes: int32 [2048, 8], P(('groups', 'node')), parts along dimension 0, may hold values from 1 to 255
- w_gate: bfloat16 [16, 4096, 768], P('node'), may hold values from -0.09375 to 0.09375
- w_up: bfloat16 [16, 4096, 768], P('node'), may hold values from -0.09375 to 0.09375
- w_down: bfloat16 [16, 768, 4096], P('node'), may hold values from -0.21875 to 0.21875
Outputs:
- mixed: bfloat16 [2048, 4096], P(('groups', 'node')), parts along dimension 0
The draws below stay inside these ranges and needn't reach their ends.
There are 2 independent parts, one for each index of `groups`. The reference program is written for one: setup_inputs(seed, part) draws one part's arguments, and reference() takes and returns one part's arrays. A program takes and returns all parts, laid end to end along the dimension named above; an argument that names none is the same for every part. Nothing has to cross between parts.
Inputs may be any that keep to these rules, and one draw needn't show every extreme that they name: `routes`: each row names 8 different experts; among the rows of one device no expert is named by more than 48 rows, a bound that some block reaches.
All inputs are finite; a program needn't handle non-finite values.
Results may differ from the reference program's by a relative error of at most 0.015.
Values may be sent and summed in bfloat16 or wider, within the bound.
No kernel may reach another device: no remote copies, remote signals or barrier semaphores. Data moves between devices by JAX's collectives and lax.ppermute only.
A program may use at most 128 MiB of HBM per device.

```python
import math
import jax
import jax.numpy as jnp
import numpy as np
from jax import lax

D = 4096
FF = 768
TOP = 8
TOK_DEV = 64
TOKENS = 1024
EXPERTS = 16
MOST = 48
N_NODE = 16


def touch_ends(entries, key, low, top_value):
    longest = entries.shape.index(max(entries.shape))
    spots = []
    for shift in (0, 1):
        where = [jax.random.randint(jax.random.fold_in(key, axis), (), 0, length) for axis, length in enumerate(entries.shape)]
        where[longest] = (where[longest] + shift) % entries.shape[longest]
        spots.append(tuple(where))
    return entries.at[spots[0]].set(low).at[spots[1]].set(top_value)


def block_levels(key, dims, split, smallest, top_value):
    def one(dim, shards_of):
        heights = jax.random.uniform(jax.random.fold_in(jax.random.fold_in(key, 6), dim), (shards_of,), jnp.float32, smallest / len(split), top_value / len(split))
        return jnp.repeat(jnp.exp(heights), dims[dim] // shards_of).reshape((-1,) + (1,) * (len(dims) - dim - 1))

    gain = one(*split[0])
    for cut in split[1:]:
        gain = gain * one(*cut)
    return gain


def assign_block(own_key, own, number, rows, count, top, reach, slope):
    ranking = jax.random.permutation(own_key, count)
    packed, usual = load_shares(count, rows * top, reach, slope, True), load_shares(count, rows * top, reach, slope, False)
    places = jnp.arange(count)

    def named(tallies, offset_by):
        used = int((tallies > 0).sum())
        fixed = max(1, used // 4)
        passed = fixed + (places - fixed + offset_by * (used - fixed)) % max(1, count - fixed)
        return jnp.zeros((count,), jnp.int32).at[ranking[jnp.where(places < fixed, places, passed)]].set(jnp.asarray(tallies, jnp.int32))

    tallies = jnp.where(number % 4 == 0, named(packed, number // 4), named(usual, number - number // 4 - 1))
    mixed = jax.random.permutation(jax.random.fold_in(own, 3), count)
    source_of, sink = mixed[0:count // 2 * 2:2], mixed[1:count // 2 * 2:2]
    margin = jnp.minimum(tallies[source_of] - 1, reach - tallies[sink]) // 2
    margin = jnp.where((source_of == ranking[0]) | (sink == ranking[0]) | (tallies[sink] == 0), 0, jnp.maximum(margin, 0))
    passed = jax.random.randint(jax.random.fold_in(own, 4), (count // 2,), 0, 1 << 20) % (margin + 1)
    tallies = tallies.at[source_of].add(-passed).at[sink].add(passed)
    members = jnp.searchsorted(jnp.cumsum(tallies), jnp.arange(rows * top), side="right").astype(jnp.int32)
    listing = members.reshape(top, rows).T
    listing = listing[jax.random.permutation(jax.random.fold_in(own, 1), rows)]
    offset_by = jax.random.randint(jax.random.fold_in(own, 2), (rows, 1), 0, top)
    return jnp.take_along_axis(listing, (jnp.arange(top)[None, :] + offset_by) % top, axis=1)


def load_shares(count, total, bound, slope, full):
    weights = [(1 << 20) // math.isqrt(rank ** slope) + 1 for rank in range(1, count + 1)]
    largest = bound if full else min(bound, max(-(-total // count), total * weights[0] // sum(weights)))
    least = 1 if total - largest >= count - 1 else 0
    holding, rest = [largest] + [least] * (count - 1), total - largest - least * (count - 1)
    while rest > 0:
        movable = [i for i in range(1, count) if holding[i] < largest] or [i for i in range(1, count) if holding[i] < bound]
        mass, budget = sum([weights[i] for i in movable]), rest
        for i in movable:
            addition = min(bound - holding[i], max(1, budget * weights[i] // mass), rest)
            holding[i] = holding[i] + addition
            rest = rest - addition
    return np.array(holding)


def centred(own_key, dims, deviation, limit, cuts=(), kind=jnp.bfloat16):
    array = deviation * jax.random.normal(own_key, dims, jnp.float32)
    if cuts:
        array = array * block_levels(own_key, dims, cuts, -0.22, 0.18)
    return jnp.clip(array, -limit, limit).astype(kind)


def setup_inputs(seed: int = 0, part: int = 0) -> dict:
    arg_keys = jax.random.split(jax.random.key(seed), 7)
    own_keys = jax.random.split(jax.random.fold_in(arg_keys[6], part), 7)
    tokens = centred(own_keys[0], (TOKENS, D), 1.0, 6.0, ((0, 16),))
    routes_keys = jax.random.split(jax.random.fold_in(own_keys[1], 1), TOKENS // TOK_DEV)
    routes_turns = jax.random.permutation(jax.random.fold_in(own_keys[1], 3), TOKENS // TOK_DEV)
    routes = jax.vmap(lambda own, number: assign_block(jax.random.fold_in(own_keys[1], 2), own, number, TOK_DEV, EXPERTS, TOP, MOST, 2))(routes_keys, routes_turns).reshape((TOKENS, TOP))
    gate_codes = touch_ends(jax.random.randint(own_keys[2], (TOKENS, TOP), 1, 256), jax.random.fold_in(own_keys[2], 1), 1, 255).astype(jnp.int32)
    w_gate = centred(arg_keys[3], (EXPERTS, D, FF), D ** -0.5, 0.09375, ((0, 16),))
    w_up = centred(arg_keys[4], (EXPERTS, D, FF), D ** -0.5, 0.09375, ((0, 16),))
    w_down = centred(arg_keys[5], (EXPERTS, FF, D), FF ** -0.5, 0.21875, ((0, 16),))
    return dict(tokens=tokens, routes=routes, gate_codes=gate_codes, w_gate=w_gate, w_up=w_up, w_down=w_down)


def quantize(tokens):
    blocks = tokens.astype(jnp.float32).reshape(tokens.shape[0], -1, 128)
    largest = jnp.max(jnp.abs(blocks), axis=-1)
    row_scales = ((largest + 1e-6) / 448.0).astype(jnp.bfloat16)
    coded_rows = (blocks / row_scales.astype(jnp.float32)[..., None]).astype(jnp.bfloat16)
    return coded_rows.reshape(tokens.shape[0], -1), row_scales


def dequantize(coded_rows, row_scales):
    blocks = coded_rows.astype(jnp.float32).reshape(coded_rows.shape[0], -1, 128)
    joined = blocks * row_scales.astype(jnp.float32)[..., None]
    return joined.astype(jnp.bfloat16).reshape(coded_rows.shape[0], -1)


def expert_forward(inputs, gate_w, up_w, down_w):
    gate = jnp.dot(inputs, gate_w, preferred_element_type=jnp.float32)
    up = jnp.dot(inputs, up_w, preferred_element_type=jnp.float32)
    hidden = (jax.nn.silu(gate) * up).astype(jnp.bfloat16)
    return jnp.dot(hidden, down_w, preferred_element_type=jnp.float32).astype(jnp.bfloat16)


def reference(tokens, routes, gate_codes, w_gate, w_up, w_down):
    coded_rows, row_scales = quantize(tokens)
    dequant_rows = dequantize(coded_rows, row_scales)
    flat_routes = routes.reshape(-1)
    pair_total = TOKENS * TOP
    capacity = N_NODE * MOST
    pair_ids = jnp.arange(pair_total, dtype=jnp.int32)

    def one_expert(carried, inputs):
        gate_w, up_w, down_w, expert = inputs
        route_mask = flat_routes == expert
        position = jnp.cumsum(route_mask.astype(jnp.int32)) - 1
        target = jnp.where(route_mask, position, capacity).astype(jnp.int32)
        slot_pair = jnp.full((capacity,), pair_total, jnp.int32).at[target].set(pair_ids, mode="drop")
        source_token = (jnp.minimum(slot_pair, pair_total - 1) // TOP).astype(jnp.int32)
        result = expert_forward(dequant_rows[source_token], gate_w, up_w, down_w)
        carried = carried.at[slot_pair].set(result, mode="drop")
        return carried, None

    start = jnp.zeros((pair_total, D), jnp.bfloat16)
    pair_out, unused = lax.scan(one_expert, start, (w_gate, w_up, w_down, jnp.arange(EXPERTS, dtype=jnp.int32)))
    codes = gate_codes.astype(jnp.float32)
    weights = codes / jnp.sum(codes, axis=1, keepdims=True)
    picked = pair_out.reshape(TOKENS, TOP, D).astype(jnp.float32)
    return jnp.sum(picked * weights[:, :, None], axis=1).astype(jnp.bfloat16)
```

```python
import functools

import jax
import jax.numpy as jnp
from jax import lax
from jax.experimental import pallas as pl
from jax.experimental.pallas import tpu as pltpu
from jax.sharding import PartitionSpec as P

LANES = 128
FF_TILE = 256
OUT_TILE = 1024


def encode_kernel(tokens_ref, routes_ref, codes_ref, first_ref, second_ref):
    rows, width = tokens_ref.shape
    half = rows // 2
    for b in range(width // LANES):
        cols = slice(b * LANES, (b + 1) * LANES)
        block = tokens_ref[:, cols].astype(jnp.float32)
        largest = jnp.max(jnp.abs(block), axis=1, keepdims=True)
        scale = ((largest + 1e-6) / 448.0).astype(jnp.bfloat16).astype(jnp.float32)
        coded = (block / scale).astype(jnp.bfloat16).astype(jnp.float32)
        value = (coded * scale).astype(jnp.bfloat16)
        first_ref[:, cols] = value[:half]
        second_ref[:, cols] = value[half:]
    lane = lax.broadcasted_iota(jnp.int32, (rows, LANES), 1)
    table = jnp.zeros((rows, LANES), jnp.float32)
    for k in range(routes_ref.shape[1]):
        code = codes_ref[:, k : k + 1].astype(jnp.float32)
        table = table + jnp.where(lane == routes_ref[:, k : k + 1], code, 0.0)
    first_ref[:, width:] = table[:half].astype(jnp.bfloat16)
    second_ref[:, width:] = table[half:].astype(jnp.bfloat16)


def encode(tokens, routes, gate_codes):
    rows, width = tokens.shape
    out = jax.ShapeDtypeStruct((rows // 2, width + LANES), jnp.bfloat16)
    return pl.pallas_call(
        encode_kernel,
        out_shape=(out, out),
        compiler_params=pltpu.CompilerParams(vmem_limit_bytes=8 << 20),
    )(tokens, routes, gate_codes)


def expert_kernel(count, me_ref, *refs):
    x_refs = refs[:count]
    gate_hbm, up_hbm, down_hbm = refs[count : count + 3]
    out_refs = refs[count + 3 : 2 * count + 3]
    gate_w, up_w, down_w, x, hidden, scale, gate_sem, up_sem, down_sem = refs[2 * count + 3 :]
    width, ff = gate_w.shape
    ff_tiles, out_tiles = ff // FF_TILE, width // OUT_TILE

    def gate_copy(t):
        cols = pl.ds(pl.multiple_of(t * FF_TILE, FF_TILE), FF_TILE)
        return (
            pltpu.make_async_copy(gate_hbm.at[:, cols], gate_w.at[:, cols], gate_sem.at[t]),
            pltpu.make_async_copy(up_hbm.at[:, cols], up_w.at[:, cols], up_sem.at[t]),
        )

    def down_copy(t):
        cols = pl.ds(pl.multiple_of(t * OUT_TILE, OUT_TILE), OUT_TILE)
        return pltpu.make_async_copy(down_hbm.at[:, cols], down_w.at[:, cols], down_sem.at[t])

    for t in range(ff_tiles):
        for copy in gate_copy(t):
            copy.start()
    for t in range(out_tiles):
        down_copy(t).start()

    lane = lax.broadcasted_iota(jnp.int32, (x_refs[0].shape[0], LANES), 1)
    for i, ref in enumerate(x_refs):
        rows = ref.shape[0]
        span = slice(i * rows, (i + 1) * rows)
        x[span, :] = ref[:, :width]
        codes = ref[:, width:].astype(jnp.float32)
        total = jnp.sum(codes, axis=1, keepdims=True)
        mine = jnp.sum(jnp.where(lane == me_ref[0], codes, 0.0), axis=1, keepdims=True)
        scale[span, :] = jnp.broadcast_to(mine / total, (rows, LANES))

    @pl.loop(0, ff_tiles)
    def _(t):
        for copy in gate_copy(t):
            copy.wait()
        cols = pl.ds(pl.multiple_of(t * FF_TILE, FF_TILE), FF_TILE)
        gate = jnp.dot(x[...], gate_w[:, cols], preferred_element_type=jnp.float32)
        up = jnp.dot(x[...], up_w[:, cols], preferred_element_type=jnp.float32)
        hidden[:, cols] = (gate / (1.0 + jnp.exp(-gate)) * up).astype(jnp.bfloat16)

    @pl.loop(0, out_tiles)
    def _(t):
        down_copy(t).wait()
        cols = pl.ds(pl.multiple_of(t * OUT_TILE, OUT_TILE), OUT_TILE)
        result = jnp.dot(hidden[...], down_w[:, cols], preferred_element_type=jnp.float32)
        for i, ref in enumerate(out_refs):
            rows = ref.shape[0]
            span = slice(i * rows, (i + 1) * rows)
            ref[:, cols] = (result[span, :] * scale[span, 0:1]).astype(jnp.bfloat16)


def expert(me, blocks, w_gate, w_up, w_down):
    count = len(blocks)
    rows = blocks[0].shape[0]
    width, ff = w_gate.shape
    total = rows * count
    out = jax.ShapeDtypeStruct((rows, width), jnp.bfloat16)
    vmem = pl.BlockSpec(memory_space=pltpu.VMEM)
    return pl.pallas_call(
        functools.partial(expert_kernel, count),
        in_specs=[pl.BlockSpec(memory_space=pltpu.SMEM)] + [vmem] * count + [pl.BlockSpec(memory_space=pl.ANY)] * 3,
        out_specs=[vmem] * count,
        out_shape=[out] * count,
        scratch_shapes=[
            pltpu.VMEM((width, ff), jnp.bfloat16),
            pltpu.VMEM((width, ff), jnp.bfloat16),
            pltpu.VMEM((ff, width), jnp.bfloat16),
            pltpu.VMEM((total, width), jnp.bfloat16),
            pltpu.VMEM((total, ff), jnp.bfloat16),
            pltpu.VMEM((total, LANES), jnp.float32),
            pltpu.SemaphoreType.DMA((ff // FF_TILE,)),
            pltpu.SemaphoreType.DMA((ff // FF_TILE,)),
            pltpu.SemaphoreType.DMA((width // OUT_TILE,)),
        ],
        cost_estimate=pl.CostEstimate(
            flops=6 * total * width * ff,
            bytes_accessed=6 * width * ff + 4 * total * width,
            transcendentals=total * ff,
        ),
        compiler_params=pltpu.CompilerParams(vmem_limit_bytes=40 << 20),
    )(me, *blocks, w_gate, w_up, w_down)


def ring_order(nodes, groups):
    chips = nodes // 2
    if groups == 2:
        return list(range(0, chips, 2)) + list(range(1, chips, 2))[::-1]
    return list(range(chips))


def local(nodes, groups, tokens, routes, gate_codes, w_gate, w_up, w_down):
    order = ring_order(nodes, groups)
    chips = len(order)
    far = chips // 2
    me = lax.axis_index("node").astype(jnp.int32).reshape(1)
    gate_w, up_w, down_w = w_gate[0], w_up[0], w_down[0]

    def hop(value, step):
        pairs = [
            (2 * order[i] + core, 2 * order[(i + step) % chips] + core) for i in range(chips) for core in (0, 1)
        ]
        return lax.ppermute(value, "node", pairs)

    def swap(value):
        return lax.ppermute(value, "node", [(i, i ^ 1) for i in range(nodes)])

    def total(*terms):
        return functools.reduce(lambda a, b: a + b, [t.astype(jnp.float32) for t in terms]).astype(jnp.bfloat16)

    held = {}
    held[0, 0], held[1, 0] = encode(tokens, routes, gate_codes)
    slots = [[(0, 0), (1, 0)]]
    for k in range(1, 2 * far):
        s = (k + 1) // 2
        ahead, behind = (0, 1) if k % 2 else (1, 0)
        held[ahead, s] = hop(held[ahead, s - 1], 1)
        held[behind, -s] = hop(held[behind, 1 - s], -1)
        slots.append([(ahead, s), (behind, -s)])
    other = {key: swap(held[key]) for slot in slots for key in slot}

    groups_of = []
    pending = []
    for k, slot in enumerate(slots):
        pending += slot
        if k % 2 or k >= 2 * far - 2:
            groups_of.append(pending)
            pending = []
    mine, theirs = {}, {}
    for keys in groups_of:
        outs = expert(me, [held[key] for key in keys] + [other[key] for key in keys], gate_w, up_w, down_w)
        for i, key in enumerate(keys):
            mine[key] = outs[i]
            theirs[key] = swap(outs[len(keys) + i])

    carried = {}
    for half in (0, 1):
        for sign in (1, -1):
            last = far if (half == 0) == (sign == 1) else far - 1
            message = None
            for s in range(last, 0, -1):
                key = (half, sign * s)
                terms = [mine[key], theirs[key]] + ([] if message is None else [message])
                message = hop(total(*terms), -sign)
            carried[half, sign] = message
    final = [
        total(mine[half, 0], theirs[half, 0], carried[half, 1], carried[half, -1]) for half in (0, 1)
    ]
    return jnp.concatenate(final, axis=0)


def solution(mesh):
    return jax.shard_map(
        functools.partial(local, mesh.shape["node"], mesh.shape["groups"]),
        mesh=mesh,
        in_specs=(
            P(("groups", "node"), None),
            P(("groups", "node"), None),
            P(("groups", "node"), None),
            P("node", None, None),
            P("node", None, None),
            P("node", None, None),
        ),
        out_specs=P(("groups", "node"), None),
        check_vma=False,
    )
```

```python
import functools

import jax
import jax.numpy as jnp
from jax import lax
from jax.experimental import pallas as pl
from jax.experimental.pallas import tpu as pltpu
from jax.sharding import PartitionSpec as P

LANES = 128
FF_TILE = 256
OUT_TILE = 512
MIB = 1 << 20


def encode_kernel(tokens_ref, routes_ref, codes_ref, out_ref):
    rows, width = tokens_ref.shape
    for b in range(width // LANES):
        cols = slice(b * LANES, (b + 1) * LANES)
        block = tokens_ref[:, cols].astype(jnp.float32)
        largest = jnp.max(jnp.abs(block), axis=1, keepdims=True)
        scale = ((largest + 1e-6) / 448.0).astype(jnp.bfloat16).astype(jnp.float32)
        coded = (block / scale).astype(jnp.bfloat16).astype(jnp.float32)
        out_ref[:, cols] = (coded * scale).astype(jnp.bfloat16)
    lane = lax.broadcasted_iota(jnp.int32, (rows, LANES), 1)
    table = jnp.zeros((rows, LANES), jnp.float32)
    for k in range(routes_ref.shape[1]):
        code = codes_ref[:, k : k + 1].astype(jnp.float32)
        table = table + jnp.where(lane == routes_ref[:, k : k + 1], code, 0.0)
    out_ref[:, width:] = table.astype(jnp.bfloat16)


def encode(tokens, routes, gate_codes):
    rows, width = tokens.shape
    return pl.pallas_call(
        encode_kernel,
        out_shape=jax.ShapeDtypeStruct((rows, width + LANES), jnp.bfloat16),
        compiler_params=pltpu.CompilerParams(vmem_limit_bytes=8 * MIB),
    )(tokens, routes, gate_codes)


def expert_kernel(count, me_ref, *refs):
    x_refs = refs[:count]
    gate_w, up_w, down_w = refs[count : count + 3]
    own_out, other_out = refs[count + 3 : count + 5]
    x, hidden, scale = refs[count + 5 :]
    width, ff = gate_w.shape
    half = own_out.shape[0]

    rows = x_refs[0].shape[0]
    lane = lax.broadcasted_iota(jnp.int32, (rows, LANES), 1)
    for i, ref in enumerate(x_refs):
        span = slice(i * rows, (i + 1) * rows)
        x[span, :] = ref[:, :width]
        codes = ref[:, width:].astype(jnp.float32)
        total = jnp.sum(codes, axis=1, keepdims=True)
        mine = jnp.sum(jnp.where(lane == me_ref[0], codes, 0.0), axis=1, keepdims=True)
        scale[span, :] = jnp.broadcast_to(mine / total, (rows, LANES))

    @pl.loop(0, ff // FF_TILE)
    def _(t):
        cols = pl.ds(pl.multiple_of(t * FF_TILE, FF_TILE), FF_TILE)
        gate = jnp.dot(x[...], gate_w[:, cols], preferred_element_type=jnp.float32)
        up = jnp.dot(x[...], up_w[:, cols], preferred_element_type=jnp.float32)
        hidden[:, cols] = (gate / (1.0 + jnp.exp(-gate)) * up).astype(jnp.bfloat16)

    @pl.loop(0, width // OUT_TILE)
    def _(t):
        cols = pl.ds(pl.multiple_of(t * OUT_TILE, OUT_TILE), OUT_TILE)
        result = jnp.dot(hidden[...], down_w[:, cols], preferred_element_type=jnp.float32)
        result = (result * scale[:, 0:1]).astype(jnp.bfloat16)
        own_out[:, cols] = result[:half]
        other_out[:, cols] = result[half:]


def expert(me, own, other, weights):
    blocks = [*own, *other]
    rows = blocks[0].shape[0]
    width, ff = weights[0].shape
    half = rows * len(own)
    out = jax.ShapeDtypeStruct((half, width), jnp.bfloat16)
    vmem = pl.BlockSpec(memory_space=pltpu.VMEM)
    pinned = [pltpu.with_memory_space_constraint(w, pltpu.VMEM) for w in weights]
    return pl.pallas_call(
        functools.partial(expert_kernel, len(blocks)),
        in_specs=[pl.BlockSpec(memory_space=pltpu.SMEM)] + [vmem] * (len(blocks) + 3),
        out_specs=[vmem, vmem],
        out_shape=[out, out],
        scratch_shapes=[
            pltpu.VMEM((2 * half, width), jnp.bfloat16),
            pltpu.VMEM((2 * half, ff), jnp.bfloat16),
            pltpu.VMEM((2 * half, LANES), jnp.float32),
        ],
        cost_estimate=pl.CostEstimate(
            flops=12 * half * width * ff,
            bytes_accessed=8 * half * width,
            transcendentals=2 * half * ff,
        ),
        compiler_params=pltpu.CompilerParams(vmem_limit_bytes=16 * MIB),
    )(me, *blocks, *pinned)


def ring_order(nodes, groups):
    chips = nodes // 2
    if groups == 2:
        return list(range(0, chips, 2)) + list(range(1, chips, 2))[::-1]
    return list(range(chips))


def after(value, *others):
    return lax.optimization_barrier((value, *others))[0]


def add(*terms):
    return functools.reduce(lambda a, b: a + b, [t.astype(jnp.float32) for t in terms])


def local(nodes, groups, tokens, routes, gate_codes, w_gate, w_up, w_down):
    order = ring_order(nodes, groups)
    chips = len(order)
    far = chips // 2
    rows = tokens.shape[0]
    node = lax.axis_index("node").astype(jnp.int32)
    first_core = (node % 2) == 0
    me = node.reshape(1)
    weights = (w_gate[0], w_up[0], w_down[0])

    def hop(value, *steps):
        steps = steps * (3 - len(steps))
        pairs = [
            (2 * order[i] + core, 2 * order[(i + steps[core]) % chips] + core)
            for i in range(chips)
            for core in (0, 1)
        ]
        return lax.ppermute(value, "node", pairs)

    def swap(value):
        return lax.ppermute(value, "node", [(i, i ^ 1) for i in range(nodes)])

    block = encode(tokens, routes, gate_codes)
    batches = [[block]]
    for s in range(1, far):
        batches.append([hop(batches[-1][0], 1), hop(batches[-1][-1], -1)])
    batches.append([hop(jnp.where(first_core, batches[-1][0], batches[-1][-1]), 1, -1)])

    mine, theirs = [], []
    for batch in batches:
        outs = expert(me, batch, [swap(b) for b in batch], weights)
        mine.append(outs[0])
        theirs.append(swap(outs[1]))

    def part(s, behind):
        span = slice(rows, None) if behind else slice(0, rows)
        return add(mine[s][span], theirs[s][span])

    low = jnp.bfloat16
    edge = hop(add(mine[far], theirs[far]).astype(low), -1, 1)
    up, down = None, None
    for s in range(far - 1, 0, -1):
        if up is None:
            up = part(s, False) + jnp.where(first_core, edge, 0).astype(jnp.float32)
            down = part(s, True) + jnp.where(first_core, 0, edge).astype(jnp.float32)
        else:
            up, down = part(s, False) + up.astype(jnp.float32), part(s, True) + down.astype(jnp.float32)
        up, down = hop(up.astype(low), -1), hop(down.astype(low), 1)
    return add(mine[0], theirs[0], up, down).astype(low)


def solution(mesh):
    return jax.shard_map(
        functools.partial(local, mesh.shape["node"], mesh.shape["groups"]),
        mesh=mesh,
        in_specs=(
            P(("groups", "node"), None),
            P(("groups", "node"), None),
            P(("groups", "node"), None),
            P("node", None, None),
            P("node", None, None),
            P("node", None, None),
        ),
        out_specs=P(("groups", "node"), None),
        check_vma=False,
    )
```

```python
import functools

import jax
import jax.numpy as jnp
from jax import lax
from jax.experimental import pallas as pl
from jax.experimental.pallas import tpu as pltpu
from jax.sharding import PartitionSpec as P

LANES = 128
FF_TILE = 256
OUT_TILE = 512
MIB = 1 << 20
LOADS = 4
SUM_FLOPS = 0
OUT_PIECES = 1
BACK_PIECES = 1


def encode_kernel(tokens_ref, routes_ref, codes_ref, *out_refs):
    rows, width = tokens_ref.shape
    part = rows // len(out_refs)
    for b in range(width // LANES):
        cols = slice(b * LANES, (b + 1) * LANES)
        block = tokens_ref[:, cols].astype(jnp.float32)
        largest = jnp.max(jnp.abs(block), axis=1, keepdims=True)
        scale = ((largest + 1e-6) / 448.0).astype(jnp.bfloat16).astype(jnp.float32)
        coded = (block / scale).astype(jnp.bfloat16).astype(jnp.float32)
        value = (coded * scale).astype(jnp.bfloat16)
        for i, ref in enumerate(out_refs):
            ref[:, cols] = value[i * part : (i + 1) * part]
    expert = lax.broadcasted_iota(jnp.int32, (LANES, rows), 0)
    table = jnp.zeros((LANES, rows), jnp.float32)
    for k in range(routes_ref.shape[0]):
        code = codes_ref[k : k + 1, :].astype(jnp.float32)
        table = table + jnp.where(expert == routes_ref[k : k + 1, :], code, 0.0)
    table = table.T.astype(jnp.bfloat16)
    for i, ref in enumerate(out_refs):
        ref[:, width:] = table[i * part : (i + 1) * part]


def encode(tokens, routes, gate_codes):
    rows, width = tokens.shape
    out = jax.ShapeDtypeStruct((rows // OUT_PIECES, width + LANES), jnp.bfloat16)
    return pl.pallas_call(
        encode_kernel,
        out_shape=[out] * OUT_PIECES,
        compiler_params=pltpu.CompilerParams(vmem_limit_bytes=8 * MIB),
    )(*[pltpu.with_memory_space_constraint(a, pltpu.HBM) for a in (tokens, routes.T, gate_codes.T)])


def expert_kernel(count, me_ref, *refs):
    x_refs = refs[:count]
    gate_w, up_w, down_w = refs[count : count + 3]
    own_out, other_out = refs[count + 3 : count + 5]
    hidden, scale = refs[count + 5 :]
    width, ff = gate_w.shape
    half = own_out.shape[0]

    rows = x_refs[0].shape[0]
    lane = lax.broadcasted_iota(jnp.int32, (rows, LANES), 1)
    for i, ref in enumerate(x_refs):
        codes = ref[:, width:].astype(jnp.float32)
        total = jnp.sum(codes, axis=1, keepdims=True)
        mine = jnp.sum(jnp.where(lane == me_ref[0], codes, 0.0), axis=1, keepdims=True)
        scale[i * rows : (i + 1) * rows, :] = jnp.broadcast_to(mine / total, (rows, LANES))

    for t in range(ff // FF_TILE):
        cols = slice(t * FF_TILE, (t + 1) * FF_TILE)
        x = jnp.concatenate([ref[:, :width] for ref in x_refs], axis=0)
        gate = jnp.dot(x, gate_w[:, cols], preferred_element_type=jnp.float32)
        up = jnp.dot(x, up_w[:, cols], preferred_element_type=jnp.float32)
        hidden[:, cols] = (gate / (1.0 + jnp.exp(-gate)) * up).astype(jnp.bfloat16)

    for t in range(width // OUT_TILE):
        cols = slice(t * OUT_TILE, (t + 1) * OUT_TILE)
        result = jnp.dot(hidden[...], down_w[:, cols], preferred_element_type=jnp.float32)
        result = (result * scale[:, 0:1]).astype(jnp.bfloat16)
        own_out[:, cols] = result[:half]
        other_out[:, cols] = result[half:]


def expert(me, own, other, weights):
    blocks = [*own, *other]
    rows = blocks[0].shape[0]
    width, ff = weights[0].shape
    half = rows * len(own)
    out = jax.ShapeDtypeStruct((half, width), jnp.bfloat16)
    vmem = pl.BlockSpec(memory_space=pltpu.VMEM)
    pinned = [pltpu.with_memory_space_constraint(w, pltpu.VMEM) for w in weights]
    return pl.pallas_call(
        functools.partial(expert_kernel, len(blocks)),
        in_specs=[pl.BlockSpec(memory_space=pltpu.SMEM)] + [vmem] * (len(blocks) + 3),
        out_specs=[vmem, vmem],
        out_shape=[out, out],
        scratch_shapes=[
            pltpu.VMEM((2 * half, ff), jnp.bfloat16),
            pltpu.VMEM((2 * half, LANES), jnp.float32),
        ],
        cost_estimate=pl.CostEstimate(
            flops=12 * half * width * ff,
            bytes_accessed=8 * half * width,
            transcendentals=2 * half * ff,
        ),
        compiler_params=pltpu.CompilerParams(vmem_limit_bytes=8 * MIB),
    )(me, *blocks, *pinned)


def load_kernel(*refs):
    count = len(refs) // 2
    copies = []
    for i in range(count):
        rows = refs[i].shape[0] // LOADS
        for j in range(LOADS):
            span = slice(j * rows, (j + 1) * rows)
            copies.append(pltpu.make_async_copy(refs[i].at[span], refs[count + i].at[span], refs[-1].at[i, j]))
    for copy in copies:
        copy.start()
    for copy in copies:
        copy.wait()


def load(weights):
    return pl.pallas_call(
        load_kernel,
        in_specs=[pl.BlockSpec(memory_space=pltpu.HBM)] * len(weights),
        out_specs=[pl.BlockSpec(memory_space=pltpu.VMEM)] * len(weights),
        out_shape=[pltpu.VMEM(w.shape, w.dtype) for w in weights],
        scratch_shapes=[pltpu.SemaphoreType.DMA((len(weights), LOADS))],
        cost_estimate=pl.CostEstimate(flops=0, bytes_accessed=sum(4 * w.size for w in weights), transcendentals=0),
        compiler_params=pltpu.CompilerParams(vmem_limit_bytes=MIB),
    )(*[pltpu.with_memory_space_constraint(w, pltpu.HBM) for w in weights])


def add_kernel(first, second, core_ref, *refs):
    ins, outs = refs[: len(refs) - len(first)], refs[len(refs) - len(first) :]
    for core, terms in ((0, first), (1, second)):

        @pl.when(core_ref[0] == core)
        def _():
            for out_ref, listed in zip(outs, terms, strict=True):
                rows = out_ref.shape[0]
                total = None
                for index, start in listed:
                    value = ins[index][start : start + rows, :].astype(jnp.float32)
                    total = value if total is None else total + value
                out_ref[...] = total.astype(out_ref.dtype)


def add_rows(core, first, second, cost):
    arrays, places = [], {}
    for sums in (first, second):
        for terms in sums:
            for array, _ in terms:
                if id(array) not in places:
                    places[id(array)] = len(arrays)
                    arrays.append(array)
    layout = [[[(places[id(array)], start) for array, start in terms] for terms in sums] for sums in (first, second)]
    vmem = pl.BlockSpec(memory_space=pltpu.VMEM)
    rows, width = cost[1]
    out = jax.ShapeDtypeStruct((rows, width), jnp.bfloat16)
    return pl.pallas_call(
        functools.partial(add_kernel, *layout),
        in_specs=[pl.BlockSpec(memory_space=pltpu.SMEM)] + [vmem] * len(arrays),
        out_specs=[vmem] * len(first),
        out_shape=[out] * len(first),
        cost_estimate=pl.CostEstimate(flops=cost[0], bytes_accessed=0, transcendentals=0),
        compiler_params=pltpu.CompilerParams(vmem_limit_bytes=4 * MIB),
    )(core, *arrays)


def ring_order(nodes, groups):
    chips = nodes // 2
    if groups == 2:
        return list(range(0, chips, 2)) + list(range(1, chips, 2))[::-1]
    return list(range(chips))


def after(values, others):
    return list(lax.optimization_barrier((*values, *others)))[: len(values)]


def local(nodes, groups, tokens, routes, gate_codes, w_gate, w_up, w_down):
    order = ring_order(nodes, groups)
    chips = len(order)
    far = chips // 2
    node = lax.axis_index("node").astype(jnp.int32)
    first_core = (node % 2) == 0
    me = node.reshape(1)
    core = (node % 2).reshape(1)

    def hop(value, *steps):
        steps = steps * (3 - len(steps))
        pairs = [
            (2 * order[i] + core, 2 * order[(i + steps[core]) % chips] + core)
            for i in range(chips)
            for core in (0, 1)
        ]
        return lax.ppermute(value, "node", pairs)

    def swap(value):
        return lax.ppermute(value, "node", [(i, i ^ 1) for i in range(nodes)])

    def pick(on_first, on_second):
        return jnp.where(first_core, on_first, on_second)

    ahead = [encode(tokens, routes, gate_codes)]
    behind = [ahead[0]]
    for _ in range(1, far):
        ahead.append([hop(piece, 1) for piece in ahead[-1]])
        behind.append([hop(piece, -1) for piece in behind[-1]])
    weights = load(after([w_gate[0], w_up[0], w_down[0]], ahead[far - 2]))
    sources = after([*ahead[-1], *behind[-1]], [weights[0]])
    last = [hop(pick(a, b), 1, -1) for a, b in zip(sources[:OUT_PIECES], sources[OUT_PIECES:], strict=True)]
    batches = [ahead[0]] + [a + b for a, b in zip(ahead[1:], behind[1:], strict=True)] + [last]

    others = [[swap(piece) for piece in batch] for batch in batches]
    sent = {}

    def run(s, *awaited):
        own = after(batches[s], awaited)
        outs = expert(me, own, others[s], weights)
        sent[s] = (outs[0], swap(outs[1]))

    shape = (tokens.shape[0] // BACK_PIECES, tokens.shape[1])

    def part(piece, s, place):
        start = (place * BACK_PIECES if 0 < s < far else 0) + piece
        return [(rows, start * shape[0]) for rows in sent[s]]

    def sums(first, second):
        return add_rows(core, first, second, (SUM_FLOPS, shape))

    pieces = range(BACK_PIECES)
    run(far)
    run(far - 1, sent[far][0])
    edges = [hop(sums([part(i, far, 0)], [part(i, far, 0)])[0], -1, 1) for i in pieces]
    moving = [(None, None)] * BACK_PIECES
    for s in range(far - 1, 0, -1):
        if s > 1:
            run(s - 1, sent[s][0])
        for i in pieces:
            up, down = [part(i, s, 0)] * 2, [part(i, s, 1)] * 2
            if s == far - 1:
                up[0], down[1] = [(edges[i], 0), *up[0]], [(edges[i], 0), *down[1]]
            else:
                up, down = [[moving[i][0], *terms] for terms in up], [[moving[i][1], *terms] for terms in down]
            totals = sums([up[0], down[0]], [up[1], down[1]])
            moving[i] = ((hop(totals[0], -1), 0), (hop(totals[1], 1), 0))
    run(0, sent[1][0])
    outs = []
    for i in pieces:
        terms = [[*moving[i], *part(i, 0, 0)]]
        outs += sums(terms, terms)
    return outs[0] if len(outs) == 1 else jnp.concatenate(outs, axis=0)


def solution(mesh):
    return jax.shard_map(
        functools.partial(local, mesh.shape["node"], mesh.shape["groups"]),
        mesh=mesh,
        in_specs=(
            P(("groups", "node"), None),
            P(("groups", "node"), None),
            P(("groups", "node"), None),
            P("node", None, None),
            P("node", None, None),
            P("node", None, None),
        ),
        out_specs=P(("groups", "node"), None),
        check_vma=False,
    )
```

```python
import functools

import jax
import jax.numpy as jnp
from jax import lax
from jax.experimental import pallas as pl
from jax.experimental.pallas import tpu as pltpu
from jax.sharding import PartitionSpec as P

LANES = 128
FF_TILE = 256
OUT_TILE = 512
MIB = 1 << 20
LOADS = 4
SUM_FLOPS = 0
OUT_PIECES = 1
BACK_PIECES = 1


def encode_kernel(tokens_ref, routes_ref, codes_ref, *out_refs):
    rows, width = tokens_ref.shape
    part = rows // len(out_refs)
    for b in range(width // LANES):
        cols = slice(b * LANES, (b + 1) * LANES)
        block = tokens_ref[:, cols].astype(jnp.float32)
        largest = jnp.max(jnp.abs(block), axis=1, keepdims=True)
        scale = ((largest + 1e-6) / 448.0).astype(jnp.bfloat16).astype(jnp.float32)
        coded = (block / scale).astype(jnp.bfloat16).astype(jnp.float32)
        value = (coded * scale).astype(jnp.bfloat16)
        for i, ref in enumerate(out_refs):
            ref[:, cols] = value[i * part : (i + 1) * part]
    expert = lax.broadcasted_iota(jnp.int32, (LANES, rows), 0)
    table = jnp.zeros((LANES, rows), jnp.float32)
    for k in range(routes_ref.shape[0]):
        code = codes_ref[k : k + 1, :].astype(jnp.float32)
        table = table + jnp.where(expert == routes_ref[k : k + 1, :], code, 0.0)
    table = table.T.astype(jnp.bfloat16)
    for i, ref in enumerate(out_refs):
        ref[:, width:] = table[i * part : (i + 1) * part]


def encode(tokens, routes, gate_codes):
    rows, width = tokens.shape
    out = jax.ShapeDtypeStruct((rows // OUT_PIECES, width + LANES), jnp.bfloat16)
    return pl.pallas_call(
        encode_kernel,
        out_shape=[out] * OUT_PIECES,
        compiler_params=pltpu.CompilerParams(vmem_limit_bytes=8 * MIB),
    )(*[pltpu.with_memory_space_constraint(a, pltpu.HBM) for a in (tokens, routes.T, gate_codes.T)])


def expert_kernel(count, me_ref, *refs):
    x_refs = refs[:count]
    gate_w, up_w, down_w = refs[count : count + 3]
    own_out, other_out = refs[count + 3 : count + 5]
    hidden, scale = refs[count + 5 :]
    width, ff = gate_w.shape
    half = own_out.shape[0]

    rows = x_refs[0].shape[0]
    lane = lax.broadcasted_iota(jnp.int32, (rows, LANES), 1)
    for i, ref in enumerate(x_refs):
        codes = ref[:, width:].astype(jnp.float32)
        total = jnp.sum(codes, axis=1, keepdims=True)
        mine = jnp.sum(jnp.where(lane == me_ref[0], codes, 0.0), axis=1, keepdims=True)
        scale[i * rows : (i + 1) * rows, :] = jnp.broadcast_to(mine / total, (rows, LANES))

    for t in range(ff // FF_TILE):
        cols = slice(t * FF_TILE, (t + 1) * FF_TILE)
        x = jnp.concatenate([ref[:, :width] for ref in x_refs], axis=0)
        gate = jnp.dot(x, gate_w[:, cols], preferred_element_type=jnp.float32)
        up = jnp.dot(x, up_w[:, cols], preferred_element_type=jnp.float32)
        hidden[:, cols] = (gate / (1.0 + jnp.exp(-gate)) * up).astype(jnp.bfloat16)

    for t in range(width // OUT_TILE):
        cols = slice(t * OUT_TILE, (t + 1) * OUT_TILE)
        result = jnp.dot(hidden[...], down_w[:, cols], preferred_element_type=jnp.float32)
        result = (result * scale[:, 0:1]).astype(jnp.bfloat16)
        own_out[:, cols] = result[:half]
        other_out[:, cols] = result[half:]


def expert(me, own, other, weights):
    blocks = [*own, *other]
    rows = blocks[0].shape[0]
    width, ff = weights[0].shape
    half = rows * len(own)
    out = jax.ShapeDtypeStruct((half, width), jnp.bfloat16)
    vmem = pl.BlockSpec(memory_space=pltpu.VMEM)
    pinned = [pltpu.with_memory_space_constraint(w, pltpu.VMEM) for w in weights]
    return pl.pallas_call(
        functools.partial(expert_kernel, len(blocks)),
        in_specs=[pl.BlockSpec(memory_space=pltpu.SMEM)] + [vmem] * (len(blocks) + 3),
        out_specs=[vmem, vmem],
        out_shape=[out, out],
        scratch_shapes=[
            pltpu.VMEM((2 * half, ff), jnp.bfloat16),
            pltpu.VMEM((2 * half, LANES), jnp.float32),
        ],
        cost_estimate=pl.CostEstimate(
            flops=12 * half * width * ff,
            bytes_accessed=8 * half * width,
            transcendentals=2 * half * ff,
        ),
        compiler_params=pltpu.CompilerParams(vmem_limit_bytes=8 * MIB),
    )(me, *blocks, *pinned)


def load_kernel(*refs):
    count = len(refs) // 2
    copies = []
    for i in range(count):
        rows = refs[i].shape[0] // LOADS
        for j in range(LOADS):
            span = slice(j * rows, (j + 1) * rows)
            copies.append(pltpu.make_async_copy(refs[i].at[span], refs[count + i].at[span], refs[-1].at[i, j]))
    for copy in copies:
        copy.start()
    for copy in copies:
        copy.wait()


def load(weights):
    return pl.pallas_call(
        load_kernel,
        in_specs=[pl.BlockSpec(memory_space=pltpu.HBM)] * len(weights),
        out_specs=[pl.BlockSpec(memory_space=pltpu.VMEM)] * len(weights),
        out_shape=[pltpu.VMEM(w.shape, w.dtype) for w in weights],
        scratch_shapes=[pltpu.SemaphoreType.DMA((len(weights), LOADS))],
        cost_estimate=pl.CostEstimate(flops=0, bytes_accessed=sum(4 * w.size for w in weights), transcendentals=0),
        compiler_params=pltpu.CompilerParams(vmem_limit_bytes=MIB),
    )(*[pltpu.with_memory_space_constraint(w, pltpu.HBM) for w in weights])


def add_kernel(first, second, core_ref, *refs):
    ins, outs = refs[: len(refs) - len(first)], refs[len(refs) - len(first) :]
    for core, terms in ((0, first), (1, second)):

        @pl.when(core_ref[0] == core)
        def _():
            for out_ref, listed in zip(outs, terms, strict=True):
                rows = out_ref.shape[0]
                total = None
                for index, start in listed:
                    value = ins[index][start : start + rows, :].astype(jnp.float32)
                    total = value if total is None else total + value
                out_ref[...] = total.astype(out_ref.dtype)


def add_rows(core, first, second, cost):
    arrays, places = [], {}
    for sums in (first, second):
        for terms in sums:
            for array, _ in terms:
                if id(array) not in places:
                    places[id(array)] = len(arrays)
                    arrays.append(array)
    layout = [[[(places[id(array)], start) for array, start in terms] for terms in sums] for sums in (first, second)]
    vmem = pl.BlockSpec(memory_space=pltpu.VMEM)
    rows, width = cost[1]
    out = jax.ShapeDtypeStruct((rows, width), jnp.bfloat16)
    return pl.pallas_call(
        functools.partial(add_kernel, *layout),
        in_specs=[pl.BlockSpec(memory_space=pltpu.SMEM)] + [vmem] * len(arrays),
        out_specs=[vmem] * len(first),
        out_shape=[out] * len(first),
        cost_estimate=pl.CostEstimate(flops=cost[0], bytes_accessed=0, transcendentals=0),
        compiler_params=pltpu.CompilerParams(vmem_limit_bytes=4 * MIB),
    )(core, *arrays)


def ring_order(nodes, groups):
    chips = nodes // 2
    if groups == 2:
        return list(range(0, chips, 2)) + list(range(1, chips, 2))[::-1]
    return list(range(chips))


def after(values, others):
    return list(lax.optimization_barrier((*values, *others)))[: len(values)]


def local(nodes, groups, tokens, routes, gate_codes, w_gate, w_up, w_down):
    order = ring_order(nodes, groups)
    chips = len(order)
    far = chips // 2
    node = lax.axis_index("node").astype(jnp.int32)
    first_core = (node % 2) == 0
    me = node.reshape(1)
    core = (node % 2).reshape(1)

    def hop(value, *steps):
        steps = steps * (3 - len(steps))
        pairs = [
            (2 * order[i] + core, 2 * order[(i + steps[core]) % chips] + core)
            for i in range(chips)
            for core in (0, 1)
        ]
        return lax.ppermute(value, "node", pairs)

    def swap(value):
        return lax.ppermute(value, "node", [(i, i ^ 1) for i in range(nodes)])

    def pick(on_first, on_second):
        return jnp.where(first_core, on_first, on_second)

    ahead = [encode(tokens, routes, gate_codes)]
    behind = [ahead[0]]
    for _ in range(1, far):
        ahead.append([hop(piece, 1) for piece in ahead[-1]])
        behind.append([hop(piece, -1) for piece in behind[-1]])
    weights = load(after([w_gate[0], w_up[0], w_down[0]], ahead[far - 2]))
    sources = after([*ahead[-1], *behind[-1]], [weights[0]])
    last = [hop(pick(a, b), 1, -1) for a, b in zip(sources[:OUT_PIECES], sources[OUT_PIECES:], strict=True)]
    batches = [ahead[0]] + [a + b for a, b in zip(ahead[1:], behind[1:], strict=True)] + [last]

    others = [[swap(piece) for piece in batch] for batch in batches]
    sent = {}

    def run(s, *awaited):
        own = after(batches[s], awaited)
        outs = expert(me, own, others[s], weights)
        sent[s] = (outs[0], swap(outs[1]))

    shape = (tokens.shape[0] // BACK_PIECES, tokens.shape[1])

    def part(piece, s, place):
        start = (place * BACK_PIECES if 0 < s < far else 0) + piece
        return [(rows, start * shape[0]) for rows in sent[s]]

    def sums(first, second):
        return add_rows(core, first, second, (SUM_FLOPS, shape))

    pieces = range(BACK_PIECES)
    run(far - 1)
    run(far, sent[far - 1][1])
    edges = [hop(sums([part(i, far, 0)], [part(i, far, 0)])[0], -1, 1) for i in pieces]
    moving = [(None, None)] * BACK_PIECES
    for s in range(far - 1, 0, -1):
        if s > 1:
            run(s - 1, sent[s][0])
        for i in pieces:
            up, down = [part(i, s, 0)] * 2, [part(i, s, 1)] * 2
            if s == far - 1:
                up[0], down[1] = [(edges[i], 0), *up[0]], [(edges[i], 0), *down[1]]
            else:
                up, down = [[moving[i][0], *terms] for terms in up], [[moving[i][1], *terms] for terms in down]
            totals = sums([up[0], down[0]], [up[1], down[1]])
            moving[i] = ((hop(totals[0], -1), 0), (hop(totals[1], 1), 0))
    run(0, sent[1][0])
    outs = []
    for i in pieces:
        terms = [[*moving[i], *part(i, 0, 0)]]
        outs += sums(terms, terms)
    return outs[0] if len(outs) == 1 else jnp.concatenate(outs, axis=0)


def solution(mesh):
    return jax.shard_map(
        functools.partial(local, mesh.shape["node"], mesh.shape["groups"]),
        mesh=mesh,
        in_specs=(
            P(("groups", "node"), None),
            P(("groups", "node"), None),
            P(("groups", "node"), None),
            P("node", None, None),
            P("node", None, None),
            P("node", None, None),
        ),
        out_specs=P(("groups", "node"), None),
        check_vma=False,
    )
```

```python
import functools

import jax
import jax.numpy as jnp
from jax import lax
from jax.experimental import pallas as pl
from jax.experimental.pallas import tpu as pltpu
from jax.sharding import PartitionSpec as P

LANES = 128
FF_TILE = 256
OUT_TILE = 1024
MIB = 1 << 20
LOADS = 4
SUM_FLOPS = 0
OUT_PIECES = 1
BACK_PIECES = 1


def encode_kernel(tokens_ref, routes_ref, codes_ref, *out_refs):
    rows, width = tokens_ref.shape
    part = rows // len(out_refs)
    for b in range(width // LANES):
        cols = slice(b * LANES, (b + 1) * LANES)
        block = tokens_ref[:, cols].astype(jnp.float32)
        largest = jnp.max(jnp.abs(block), axis=1, keepdims=True)
        scale = ((largest + 1e-6) / 448.0).astype(jnp.bfloat16).astype(jnp.float32)
        coded = (block / scale).astype(jnp.bfloat16).astype(jnp.float32)
        value = (coded * scale).astype(jnp.bfloat16)
        for i, ref in enumerate(out_refs):
            ref[:, cols] = value[i * part : (i + 1) * part]
    expert = lax.broadcasted_iota(jnp.int32, (LANES, rows), 0)
    table = jnp.zeros((LANES, rows), jnp.float32)
    for k in range(routes_ref.shape[0]):
        code = codes_ref[k : k + 1, :].astype(jnp.float32)
        table = table + jnp.where(expert == routes_ref[k : k + 1, :], code, 0.0)
    table = table.T.astype(jnp.bfloat16)
    for i, ref in enumerate(out_refs):
        ref[:, width:] = table[i * part : (i + 1) * part]


def encode(tokens, routes, gate_codes):
    rows, width = tokens.shape
    out = jax.ShapeDtypeStruct((rows // OUT_PIECES, width + LANES), jnp.bfloat16)
    return pl.pallas_call(
        encode_kernel,
        out_shape=[out] * OUT_PIECES,
        compiler_params=pltpu.CompilerParams(vmem_limit_bytes=8 * MIB),
    )(*[pltpu.with_memory_space_constraint(a, pltpu.HBM) for a in (tokens, routes.T, gate_codes.T)])


def expert_kernel(count, me_ref, *refs):
    x_refs = refs[:count]
    gate_w, up_w, down_w = refs[count : count + 3]
    own_out, other_out = refs[count + 3 : count + 5]
    hidden, scale = refs[count + 5 :]
    width, ff = gate_w.shape
    half = own_out.shape[0]

    rows = x_refs[0].shape[0]
    lane = lax.broadcasted_iota(jnp.int32, (rows, LANES), 1)
    for i, ref in enumerate(x_refs):
        codes = ref[:, width:].astype(jnp.float32)
        total = jnp.sum(codes, axis=1, keepdims=True)
        mine = jnp.sum(jnp.where(lane == me_ref[0], codes, 0.0), axis=1, keepdims=True)
        scale[i * rows : (i + 1) * rows, :] = jnp.broadcast_to(mine / total, (rows, LANES))

    for t in range(ff // FF_TILE):
        cols = slice(t * FF_TILE, (t + 1) * FF_TILE)
        x = jnp.concatenate([ref[:, :width] for ref in x_refs], axis=0)
        gate = jnp.dot(x, gate_w[:, cols], preferred_element_type=jnp.float32)
        up = jnp.dot(x, up_w[:, cols], preferred_element_type=jnp.float32)
        hidden[:, cols] = (gate / (1.0 + jnp.exp(-gate)) * up).astype(jnp.bfloat16)

    for t in range(width // OUT_TILE):
        cols = slice(t * OUT_TILE, (t + 1) * OUT_TILE)
        result = jnp.dot(hidden[...], down_w[:, cols], preferred_element_type=jnp.float32)
        result = (result * scale[:, 0:1]).astype(jnp.bfloat16)
        own_out[:, cols] = result[:half]
        other_out[:, cols] = result[half:]


def expert(me, own, other, weights):
    blocks = [*own, *other]
    rows = blocks[0].shape[0]
    width, ff = weights[0].shape
    half = rows * len(own)
    out = jax.ShapeDtypeStruct((half, width), jnp.bfloat16)
    vmem = pl.BlockSpec(memory_space=pltpu.VMEM)
    pinned = [pltpu.with_memory_space_constraint(w, pltpu.VMEM) for w in weights]
    return pl.pallas_call(
        functools.partial(expert_kernel, len(blocks)),
        in_specs=[pl.BlockSpec(memory_space=pltpu.SMEM)] + [vmem] * (len(blocks) + 3),
        out_specs=[vmem, vmem],
        out_shape=[out, out],
        scratch_shapes=[
            pltpu.VMEM((2 * half, ff), jnp.bfloat16),
            pltpu.VMEM((2 * half, LANES), jnp.float32),
        ],
        cost_estimate=pl.CostEstimate(
            flops=12 * half * width * ff,
            bytes_accessed=8 * half * width,
            transcendentals=2 * half * ff,
        ),
        compiler_params=pltpu.CompilerParams(vmem_limit_bytes=8 * MIB),
    )(me, *blocks, *pinned)


def load_kernel(*refs):
    count = len(refs) // 2
    copies = []
    for i in range(count):
        rows = refs[i].shape[0] // LOADS
        for j in range(LOADS):
            span = slice(j * rows, (j + 1) * rows)
            copies.append(pltpu.make_async_copy(refs[i].at[span], refs[count + i].at[span], refs[-1].at[i, j]))
    for copy in copies:
        copy.start()
    for copy in copies:
        copy.wait()


def load(weights):
    return pl.pallas_call(
        load_kernel,
        in_specs=[pl.BlockSpec(memory_space=pltpu.HBM)] * len(weights),
        out_specs=[pl.BlockSpec(memory_space=pltpu.VMEM)] * len(weights),
        out_shape=[pltpu.VMEM(w.shape, w.dtype) for w in weights],
        scratch_shapes=[pltpu.SemaphoreType.DMA((len(weights), LOADS))],
        cost_estimate=pl.CostEstimate(flops=0, bytes_accessed=sum(4 * w.size for w in weights), transcendentals=0),
        compiler_params=pltpu.CompilerParams(vmem_limit_bytes=MIB),
    )(*[pltpu.with_memory_space_constraint(w, pltpu.HBM) for w in weights])


def add_kernel(first, second, core_ref, *refs):
    ins, outs = refs[: len(refs) - len(first)], refs[len(refs) - len(first) :]
    for core, terms in ((0, first), (1, second)):

        @pl.when(core_ref[0] == core)
        def _():
            for out_ref, listed in zip(outs, terms, strict=True):
                rows = out_ref.shape[0]
                total = None
                for index, start in listed:
                    value = ins[index][start : start + rows, :].astype(jnp.float32)
                    total = value if total is None else total + value
                out_ref[...] = total.astype(out_ref.dtype)


def add_rows(core, first, second, cost):
    arrays, places = [], {}
    for sums in (first, second):
        for terms in sums:
            for array, _ in terms:
                if id(array) not in places:
                    places[id(array)] = len(arrays)
                    arrays.append(array)
    layout = [[[(places[id(array)], start) for array, start in terms] for terms in sums] for sums in (first, second)]
    vmem = pl.BlockSpec(memory_space=pltpu.VMEM)
    rows, width = cost[1]
    out = jax.ShapeDtypeStruct((rows, width), jnp.bfloat16)
    return pl.pallas_call(
        functools.partial(add_kernel, *layout),
        in_specs=[pl.BlockSpec(memory_space=pltpu.SMEM)] + [vmem] * len(arrays),
        out_specs=[vmem] * len(first),
        out_shape=[out] * len(first),
        cost_estimate=pl.CostEstimate(flops=cost[0], bytes_accessed=0, transcendentals=0),
        compiler_params=pltpu.CompilerParams(vmem_limit_bytes=4 * MIB),
    )(core, *arrays)


def ring_order(nodes, groups):
    chips = nodes // 2
    if groups == 2:
        return list(range(0, chips, 2)) + list(range(1, chips, 2))[::-1]
    return list(range(chips))


def after(values, others):
    return list(lax.optimization_barrier((*values, *others)))[: len(values)]


def local(nodes, groups, tokens, routes, gate_codes, w_gate, w_up, w_down):
    order = ring_order(nodes, groups)
    chips = len(order)
    far = chips // 2
    node = lax.axis_index("node").astype(jnp.int32)
    first_core = (node % 2) == 0
    me = node.reshape(1)
    core = (node % 2).reshape(1)

    def hop(value, *steps):
        steps = steps * (3 - len(steps))
        pairs = [
            (2 * order[i] + core, 2 * order[(i + steps[core]) % chips] + core)
            for i in range(chips)
            for core in (0, 1)
        ]
        return lax.ppermute(value, "node", pairs)

    def swap(value):
        return lax.ppermute(value, "node", [(i, i ^ 1) for i in range(nodes)])

    def pick(on_first, on_second):
        return jnp.where(first_core, on_first, on_second)

    ahead = [encode(tokens, routes, gate_codes)]
    behind = [ahead[0]]
    for _ in range(1, far):
        ahead.append([hop(piece, 1) for piece in ahead[-1]])
        behind.append([hop(piece, -1) for piece in behind[-1]])
    weights = load(after([w_gate[0], w_up[0], w_down[0]], ahead[far - 2]))
    sources = after([*ahead[-1], *behind[-1]], [weights[0]])
    last = [hop(pick(a, b), 1, -1) for a, b in zip(sources[:OUT_PIECES], sources[OUT_PIECES:], strict=True)]
    batches = [ahead[0]] + [a + b for a, b in zip(ahead[1:], behind[1:], strict=True)] + [last]

    others = [[swap(piece) for piece in batch] for batch in batches]
    sent = {}

    def run(s, *awaited):
        own = after(batches[s], awaited)
        outs = expert(me, own, others[s], weights)
        sent[s] = (outs[0], swap(outs[1]))

    shape = (tokens.shape[0] // BACK_PIECES, tokens.shape[1])

    def part(piece, s, place):
        start = (place * BACK_PIECES if 0 < s < far else 0) + piece
        return [(rows, start * shape[0]) for rows in sent[s]]

    def sums(first, second):
        return add_rows(core, first, second, (SUM_FLOPS, shape))

    pieces = range(BACK_PIECES)
    run(far - 1)
    run(far, sent[far - 1][1])
    edges = [hop(sums([part(i, far, 0)], [part(i, far, 0)])[0], -1, 1) for i in pieces]
    moving = [(None, None)] * BACK_PIECES
    for s in range(far - 1, 0, -1):
        if s > 1:
            run(s - 1, sent[s][0])
        for i in pieces:
            up, down = [part(i, s, 0)] * 2, [part(i, s, 1)] * 2
            if s == far - 1:
                up[0], down[1] = [(edges[i], 0), *up[0]], [(edges[i], 0), *down[1]]
            else:
                up, down = [[moving[i][0], *terms] for terms in up], [[moving[i][1], *terms] for terms in down]
            totals = sums([up[0], down[0]], [up[1], down[1]])
            moving[i] = ((hop(totals[0], -1), 0), (hop(totals[1], 1), 0))
    run(0, sent[1][0])
    outs = []
    for i in pieces:
        terms = [[*moving[i], *part(i, 0, 0)]]
        outs += sums(terms, terms)
    return outs[0] if len(outs) == 1 else jnp.concatenate(outs, axis=0)


def solution(mesh):
    return jax.shard_map(
        functools.partial(local, mesh.shape["node"], mesh.shape["groups"]),
        mesh=mesh,
        in_specs=(
            P(("groups", "node"), None),
            P(("groups", "node"), None),
            P(("groups", "node"), None),
            P("node", None, None),
            P("node", None, None),
            P("node", None, None),
        ),
        out_specs=P(("groups", "node"), None),
        check_vma=False,
    )
```
